512 devices in a mesh: section: 8 (over x, core), neuron: 64 (over z, y).
Axes of the slice: x: 4, y: 8, z: 8, core: 2. Of those that a mesh axis runs over, the one named last changes fastest.
Arguments:
- features: bfloat16 [128, 65536], P('section', 'neuron'), may hold values from 0 to 16
- tiles: bfloat16 [8, 16384, 4096], P('section', 'neuron'), may hold values from -0.3125 to 0.3125
- tile_row: int32 [8, 16384], P('section'), may hold values from 0 to 1023, as said below
- tile_col: int32 [8, 16384], P('section', 'neuron'), may hold values from 0 to 15
- tile_count: int32 [8, 64], P('section'), may hold values from 128 to 256, as said below
- bias: float32 [8, 65536], P('section', 'neuron'), may hold values from -0.9 to 0
Outputs:
- activations: bfloat16 [128, 65536], P('section', 'neuron')
The draws below stay inside these ranges and needn't reach their ends.
Inputs may be any that keep to these rules, and one draw needn't show every extreme that they name: `tile_row`: tile g of a layer belongs to shard g // 256. Among the used tiles of one shard in one layer, those reading blocks of one shard (block // 16) read at most 2 distinct blocks; in every layer some shard reads exactly 2 distinct blocks of every shard. The used tiles of a shard are its first tile_count slots; every layer has a shard with all 256 used.
All inputs are finite; a program needn't handle non-finite values.
Results may differ from the reference program's by a relative error of at most 0.02.
Values may be sent and summed in bfloat16 or wider, within the bound.
No kernel may reach another device: no remote copies, remote signals or barrier semaphores. Data moves between devices by JAX's collectives and lax.ppermute only.
A program may use at most 64 MiB of HBM per device.

```python
import jax
import jax.numpy as jnp
from jax import lax

BS = 64
BLK_DEV = 16
TILES = 256
NEURONS = 65536
NBLK = 1024
CAP = 2
LAYERS = 8
ROWS = 128
N_NEURON = 64


def pattern_draw(key):
    key_perm, key_cand, key_count, key_full, key_pick = jax.random.split(key, 5)
    groups = LAYERS * N_NEURON
    sources = jax.vmap(lambda subkey: jax.random.permutation(subkey, N_NEURON))(jax.random.split(key_perm, groups))
    sources = sources.reshape(LAYERS, N_NEURON, N_NEURON).astype(jnp.int32)
    local_sets = jax.vmap(lambda subkey: jax.random.permutation(subkey, BLK_DEV)[:CAP])(jax.random.split(key_cand, groups * N_NEURON))
    local_sets = local_sets.reshape(LAYERS, N_NEURON, N_NEURON * CAP).astype(jnp.int32)
    counts = jax.random.randint(key_count, (LAYERS, N_NEURON), TILES // 2, TILES + 1).astype(jnp.int32)
    full_owner = jax.random.randint(key_full, (LAYERS, 1), 0, N_NEURON)
    is_full = jnp.arange(N_NEURON)[None, :] == full_owner
    counts = jnp.where(is_full, TILES, counts).astype(jnp.int32)
    slot_ids = jnp.arange(TILES, dtype=jnp.int32)
    spread = slot_ids // N_NEURON % CAP
    chosen = jax.random.randint(key_pick, (LAYERS, N_NEURON, TILES), 0, CAP).astype(jnp.int32)
    chosen = jnp.where(is_full[:, :, None], spread[None, None, :], chosen)
    cycle = jnp.broadcast_to(slot_ids % N_NEURON, (LAYERS, N_NEURON, TILES))
    anchor = jnp.take_along_axis(sources, cycle, axis=2)
    local_block = jnp.take_along_axis(local_sets, anchor * CAP + chosen, axis=2)
    tile_rows = (anchor * BLK_DEV + local_block).reshape(LAYERS, N_NEURON * TILES).astype(jnp.int32)
    return (tile_rows, counts)


def draw_tile_row(key, part):
    tile_rows, counts = pattern_draw(key)
    return tile_rows


def draw_tile_count(key, part):
    tile_rows, counts = pattern_draw(key)
    return counts


def touch_ends(entries, key, least, high):
    dims = entries.shape
    index_at = [jax.random.randint(jax.random.fold_in(key, axis), (), 0, dims[axis]) for axis in range(len(dims))]
    entries = entries.at[tuple(index_at)].set(least)
    longest = dims.index(max(dims))
    index_at[longest] = (index_at[longest] + 1) % dims[longest]
    return entries.at[tuple(index_at)].set(high)


def level_of(key, shape, cuts, least, high):
    def one(dim, shards_of):
        draws = jax.random.uniform(jax.random.fold_in(jax.random.fold_in(key, 6), dim), (shards_of,), jnp.float32, least / len(cuts), high / len(cuts))
        return jnp.repeat(jnp.exp(draws), shape[dim] // shards_of).reshape((-1,) + (1,) * (len(shape) - dim - 1))

    gain = one(*cuts[0])
    for cut in cuts[1:]:
        gain = gain * one(*cut)
    return gain


def centred(rng, shape, scale, bound, pieces=(), kind=jnp.bfloat16):
    values = scale * jax.random.normal(rng, shape, jnp.float32)
    if pieces:
        values = values * level_of(rng, shape, pieces, -0.22, 0.18)
    return jnp.clip(values, -bound, bound).astype(kind)


def setup_inputs(seed: int = 0) -> dict:
    key_of = jax.random.split(jax.random.key(seed), 7)
    features = jnp.clip(16.0 * jax.random.uniform(key_of[0], (ROWS, NEURONS), jnp.float32) ** level_of(key_of[0], (ROWS, NEURONS), ((0, 8), (1, 64)), -0.2, 0.2), 0.0, 16.0).astype(jnp.bfloat16)
    tiles = centred(key_of[1], (LAYERS, N_NEURON * TILES, BS * BS), (3 * TILES * BS // (8 * BLK_DEV)) ** -0.5, 0.3125, ((0, 8), (1, 64)))
    tile_row = draw_tile_row(jax.random.fold_in(key_of[6], 71), 0)
    tile_col = touch_ends(jax.random.randint(key_of[3], (LAYERS, N_NEURON * TILES), 0, BLK_DEV), jax.random.fold_in(key_of[3], 1), 0, BLK_DEV - 1).astype(jnp.int32)
    tile_count = draw_tile_count(jax.random.fold_in(key_of[6], 71), 0)
    bias = jnp.clip(-0.9 + 0.9 * jax.random.uniform(key_of[5], (LAYERS, NEURONS), jnp.float32) ** level_of(key_of[5], (LAYERS, NEURONS), ((0, 8), (1, 64)), -0.2, 0.2), -0.9, 0.0)
    return dict(features=features, tiles=tiles, tile_row=tile_row, tile_col=tile_col, tile_count=tile_count, bias=bias)


CLAMP_TOP = 32.0


def reference(features, tiles, tile_row, tile_col, tile_count, bias):
    row_count = features.shape[0]
    activation = features
    for layer_index in range(LAYERS):
        blocks = activation.astype(jnp.float32).reshape(row_count, NBLK, BS)

        def owner_term(owner):
            first_tile = owner * TILES
            owned_rows = lax.dynamic_slice_in_dim(tile_row[layer_index], first_tile, TILES)
            owned_cols = lax.dynamic_slice_in_dim(tile_col[layer_index], first_tile, TILES)
            owned_tiles = lax.dynamic_slice_in_dim(tiles[layer_index], first_tile, TILES).reshape(TILES, BS, BS).astype(jnp.float32)
            used_mask = (jnp.arange(TILES, dtype=jnp.int32) < tile_count[layer_index, owner]).astype(jnp.float32)
            inputs = jnp.take(blocks, owned_rows, axis=1)
            partial_value = jnp.einsum("rki,kio->rko", inputs, owned_tiles, precision=lax.Precision.HIGHEST)
            onehot = (owned_cols[:, None] == jnp.arange(BLK_DEV, dtype=jnp.int32)[None, :]).astype(jnp.float32)
            onehot = onehot * used_mask[:, None]
            return jnp.einsum("rko,kc->rco", partial_value, onehot, precision=lax.Precision.HIGHEST)

        owner_terms = lax.map(owner_term, jnp.arange(N_NEURON, dtype=jnp.int32))
        totals = jnp.transpose(owner_terms, (1, 0, 2, 3)).reshape(row_count, NEURONS) + bias[layer_index]
        activation = jnp.clip(totals, 0.0, CLAMP_TOP).astype(jnp.bfloat16)
    return activation
```

```python
import functools

import jax
import jax.numpy as jnp
from jax import lax
from jax.experimental import pallas as pl
from jax.experimental.pallas import tpu as pltpu
from jax.sharding import PartitionSpec as P

BS = 64
CLAMP_TOP = 32.0
LANES = 128
GROUP = 8
INDEX_ROWS = 5


def reorder_kernel(in_ref, out_ref):
    groups = out_ref.shape[0]
    half = in_ref.shape[1]
    low = lax.broadcasted_iota(jnp.int32, (half, LANES), 1) < BS
    for group in range(groups):
        for pair in range(GROUP // 2):
            first = in_ref[group * GROUP + 2 * pair].astype(jnp.float32)
            second = in_ref[group * GROUP + 2 * pair + 1].astype(jnp.float32)
            even = jnp.where(low, first, pltpu.roll(second, BS, 1))
            odd = jnp.where(low, pltpu.roll(first, BS, 1), second)
            at = pair * 2 * half
            out_ref[group, at : at + half, :] = even.astype(out_ref.dtype)
            out_ref[group, at + half : at + 2 * half, :] = odd.astype(out_ref.dtype)


def reorder_tiles(slabs):
    tiles, half, _ = slabs.shape
    steps = 4
    per_step = tiles // steps
    return pl.pallas_call(
        reorder_kernel,
        grid=(steps,),
        in_specs=[pl.BlockSpec((per_step, half, LANES), lambda i: (i, 0, 0))],
        out_specs=pl.BlockSpec((per_step // GROUP, GROUP * half, LANES), lambda i: (i, 0, 0)),
        out_shape=jax.ShapeDtypeStruct((tiles // GROUP, GROUP * half, LANES), slabs.dtype),
        name="reorder_tiles",
    )(slabs)


def parity_position(lane):
    within = lane % BS
    return 2 * (within % (BS // 2)) + within // (BS // 2)


def spread_matrix(offset):
    row = lax.broadcasted_iota(jnp.int32, (LANES, 2 * LANES), 0)
    col = lax.broadcasted_iota(jnp.int32, (LANES, 2 * LANES), 1)
    lane = col % LANES
    wanted_half = (col // LANES) == (lane // BS)
    hit = wanted_half & (row == parity_position(lane) + offset)
    return hit.astype(jnp.float32).astype(jnp.bfloat16)


def pack_blocks(index_ref, pick_at, low_ref, high_ref, out_ref):
    shards = out_ref.shape[0]
    for shard in range(shards):
        first = index_ref[pick_at + shard]
        second = index_ref[pick_at + shards + shard]
        out_ref[shard] = low_ref[first] + high_ref[second]


def first_pack_kernel(pick_at, index_ref, in_ref, out_ref, low_ref, high_ref):
    rows, width = in_ref.shape
    for offset in range(2):
        spread = spread_matrix(offset * BS)
        for tile in range(width // LANES):
            value = jnp.dot(
                in_ref[:, tile * LANES : (tile + 1) * LANES], spread, preferred_element_type=jnp.float32
            ).astype(jnp.bfloat16)
            low_ref[2 * tile + offset] = value[:, :LANES]
            high_ref[2 * tile + offset] = value[:, LANES:]
    pack_blocks(index_ref, pick_at, low_ref, high_ref, out_ref)


def first_pack(index, features, shards, pick_at):
    rows, width = features.shape
    blocks = width // BS
    return pl.pallas_call(
        functools.partial(first_pack_kernel, pick_at),
        grid_spec=pltpu.PrefetchScalarGridSpec(
            num_scalar_prefetch=1,
            grid=(1,),
            in_specs=[pl.BlockSpec((rows, width), lambda i, index: (0, 0))],
            out_specs=pl.BlockSpec((shards, rows, LANES), lambda i, index: (0, 0, 0)),
            scratch_shapes=[pltpu.VMEM((blocks, rows, LANES), jnp.bfloat16)] * 2,
        ),
        out_shape=jax.ShapeDtypeStruct((shards, rows, LANES), jnp.bfloat16),
        name="first_pack",
    )(index, features)


def layer_kernel(index_at, pick_at, index_ref, in_ref, tiles_ref, bias_ref, out_ref, spread_ref, total_ref, low_ref, high_ref):
    step = pl.program_id(0)
    steps = pl.num_programs(0)
    shards, rows, _ = in_ref.shape
    groups = tiles_ref.shape[0]
    tile_slots = groups * GROUP * steps
    blocks = total_ref.shape[1] - 1

    @pl.when(step == 0)
    def _():
        total_ref[...] = jnp.zeros_like(total_ref)
        low = lax.broadcasted_iota(jnp.int32, (rows, LANES), 1) < BS
        for shard in range(shards):
            value = in_ref[shard].astype(jnp.float32)
            turned = pltpu.roll(value, BS, 1)
            spread_ref[0, 2 * shard] = jnp.where(low, value, 0.0).astype(jnp.bfloat16)
            spread_ref[0, 2 * shard + 1] = jnp.where(low, turned, 0.0).astype(jnp.bfloat16)
            spread_ref[1, 2 * shard] = jnp.where(low, 0.0, turned).astype(jnp.bfloat16)
            spread_ref[1, 2 * shard + 1] = jnp.where(low, 0.0, value).astype(jnp.bfloat16)

    empty = jnp.zeros((rows, LANES), jnp.bfloat16)
    for group in range(groups):
        first_tile = (step * groups + group) * GROUP
        left = []
        right = []
        for member in range(GROUP):
            pair = member // 2
            slot = index_ref[index_at + first_tile + member]
            value = spread_ref[pair % 2, slot]
            left.append(value if pair < 2 else empty)
            right.append(value if pair >= 2 else empty)
        gathered = jnp.concatenate([jnp.concatenate(left, axis=0), jnp.concatenate(right, axis=0)], axis=1)
        product = jnp.dot(gathered, tiles_ref[group], preferred_element_type=jnp.float32)
        for member in range(GROUP):
            column = index_ref[index_at + tile_slots + first_tile + member]
            total_ref[member % 2, column] += product[member * rows : (member + 1) * rows]

    @pl.when(step == steps - 1)
    def _():
        even = total_ref[0, :blocks].reshape(blocks * rows, LANES)
        odd = total_ref[1, :blocks].reshape(blocks * rows, LANES)
        summed = (even + pltpu.roll(odd, BS, 1)).reshape(blocks, rows, LANES) + bias_ref[...][:, None, :]
        result = jnp.clip(summed, 0.0, CLAMP_TOP)
        if pick_at is None:
            low = lax.broadcasted_iota(jnp.int32, (rows, LANES), 1) < BS
            for tile in range(blocks // 2):
                value = jnp.where(low, result[2 * tile], pltpu.roll(result[2 * tile + 1], BS, 1))
                out_ref[:, tile * LANES : (tile + 1) * LANES] = value.astype(out_ref.dtype)
        else:
            value = jnp.dot(
                result.astype(jnp.bfloat16).reshape(blocks * rows, LANES),
                spread_matrix(0),
                preferred_element_type=jnp.float32,
            ).astype(jnp.bfloat16)
            low_ref[...] = value[:, :LANES].reshape(blocks, rows, LANES)
            high_ref[...] = value[:, LANES:].reshape(blocks, rows, LANES)
            pack_blocks(index_ref, pick_at, low_ref, high_ref, out_ref)


def run_layer(index, incoming, weights, bias, layer, blocks, last):
    shards, rows, _ = incoming.shape
    groups, depth = weights.shape[1:3]
    tile_slots = groups * GROUP
    steps = 4
    stride = INDEX_ROWS * LANES
    pick_at = None if last else (layer + 1) * stride + 2 * tile_slots
    if last:
        out_shape = (rows, blocks * BS)
    else:
        out_shape = (shards, rows, LANES)
    zeros = (0,) * len(out_shape)
    return pl.pallas_call(
        functools.partial(layer_kernel, layer * stride, pick_at),
        grid_spec=pltpu.PrefetchScalarGridSpec(
            num_scalar_prefetch=1,
            grid=(steps,),
            in_specs=[
                pl.BlockSpec((shards, rows, LANES), lambda i, index: (0, 0, 0)),
                pl.BlockSpec((None, groups // steps, depth, LANES), lambda i, index: (layer, i, 0, 0)),
                pl.BlockSpec((None, blocks, LANES), lambda i, index: (layer, 0, 0)),
            ],
            out_specs=pl.BlockSpec(out_shape, lambda i, index: zeros),
            scratch_shapes=[
                pltpu.VMEM((2, 2 * shards, rows, LANES), jnp.bfloat16),
                pltpu.VMEM((2, blocks + 1, rows, LANES), jnp.float32),
                pltpu.VMEM((blocks, rows, LANES), jnp.bfloat16),
                pltpu.VMEM((blocks, rows, LANES), jnp.bfloat16),
            ],
        ),
        out_shape=jax.ShapeDtypeStruct(out_shape, jnp.bfloat16),
        name="layer_step",
    )(index, incoming, weights, bias)


def plan_routes(tile_row, tile_col, tile_count, own_index, blocks_dev):
    shards = tile_count.shape[0]
    tile_slots = tile_col.shape[0]
    slot_ids = jnp.arange(tile_slots, dtype=jnp.int32)
    rows = tile_row.reshape(shards, tile_slots)
    own_rows = lax.dynamic_index_in_dim(rows, own_index, 0, keepdims=False)
    own_used = slot_ids < tile_count[own_index]
    own_shards = own_rows // blocks_dev
    earlier = (own_shards[None, :] == own_shards[:, None]) & (own_rows[None, :] < own_rows[:, None]) & own_used[None, :]
    rank = jnp.any(earlier, axis=1).astype(jnp.int32)
    slot = jnp.where(own_used, 2 * own_shards + rank, 0)
    column = jnp.where(own_used, tile_col, blocks_dev)
    wanted = (rows // blocks_dev == own_index) & (slot_ids[None, :] < tile_count[:, None])
    local = rows - own_index * blocks_dev
    lowest = jnp.min(jnp.where(wanted, local, blocks_dev - 1), axis=1)
    highest = jnp.max(jnp.where(wanted, local, 0), axis=1)
    return jnp.concatenate([slot, column, lowest, highest])


def body(features, tiles, tile_row, tile_col, tile_count, bias):
    shards = lax.axis_size("neuron")
    layers = lax.axis_size("section")
    own_index = lax.axis_index("neuron")
    rows, width = features.shape
    blocks = width // BS
    tile_slots = tiles.shape[1]
    with jax.named_scope("tile_order"):
        slabs = tiles[0].reshape(tile_slots, BS * BS // LANES, LANES)
        ordered = reorder_tiles(slabs)
    with jax.named_scope("weight_gather"):
        weights = lax.all_gather(ordered, "section", axis=0)
    with jax.named_scope("routes"):
        routes = plan_routes(tile_row[0], tile_col[0], tile_count[0], own_index, blocks)
        own = jnp.concatenate(
            [
                routes.astype(jnp.float32).reshape(INDEX_ROWS, LANES),
                jnp.zeros((8 - INDEX_ROWS, LANES), jnp.float32),
                bias[0].reshape(width // LANES, LANES),
            ]
        )
        shared = lax.all_to_all(jnp.broadcast_to(own[None], (layers,) + own.shape), "section", 0, 0, tiled=True)
        index = shared[:, :INDEX_ROWS].astype(jnp.int32).reshape(-1)
        biases = shared[:, 8:].reshape(layers, blocks, BS)
        biases = jnp.pad(biases, ((0, 0), (0, 0), (0, LANES - BS)))
    with jax.named_scope("layers"):
        outgoing = first_pack(index, features, shards, 2 * tile_slots)
        for layer in range(layers):
            incoming = lax.all_to_all(outgoing, "neuron", 0, 0, tiled=True)
            outgoing = run_layer(index, incoming, weights, biases, layer, blocks, layer == layers - 1)
    return outgoing


def solution(mesh):
    in_specs = (
        P("section", "neuron"),
        P("section", "neuron", None),
        P("section", None),
        P("section", "neuron"),
        P("section", None),
        P("section", "neuron"),
    )
    out_specs = P("section", "neuron")
    return jax.shard_map(body, mesh=mesh, in_specs=in_specs, out_specs=out_specs, check_vma=False)
```

```python
import functools

import jax
import jax.numpy as jnp
from jax import lax
from jax.experimental import pallas as pl
from jax.experimental.pallas import tpu as pltpu
from jax.sharding import PartitionSpec as P

BS = 64
CLAMP_TOP = 32.0
LANES = 128
GROUP = 8
INDEX_STRIDE = 1024
PICKS_AT = 512
VMEM_LIMIT = 48 << 20


def reorder_kernel(in_ref, out_ref, move_ref):
    groups, depth, _ = in_ref.shape
    half = depth // GROUP
    pairs = GROUP // 2

    @pl.when(pl.program_id(0) == 0)
    def _():
        row = lax.broadcasted_iota(jnp.int32, (depth, depth), 0)
        col = lax.broadcasted_iota(jnp.int32, (depth, depth), 1)
        parity = row // (pairs * half)
        pair = row // half % pairs
        slab = row % half
        hit = col == slab * GROUP + 2 * pair + parity
        move_ref[...] = hit.astype(jnp.float32).astype(jnp.bfloat16)

    low = lax.broadcasted_iota(jnp.int32, (half, LANES), 1) < BS
    for group in range(groups):
        moved = jnp.dot(move_ref[...], in_ref[group], preferred_element_type=jnp.float32)
        for pair in range(pairs):
            first = moved[pair * half : (pair + 1) * half]
            second = moved[(pairs + pair) * half : (pairs + pair + 1) * half]
            even = jnp.where(low, first, pltpu.roll(second, BS, 1))
            odd = jnp.where(low, pltpu.roll(first, BS, 1), second)
            at = pair * 2 * half
            out_ref[group, at : at + half, :] = even.astype(out_ref.dtype)
            out_ref[group, at + half : at + 2 * half, :] = odd.astype(out_ref.dtype)


def reorder_tiles(bands):
    groups, depth, _ = bands.shape
    steps = 4
    block = pl.BlockSpec((groups // steps, depth, LANES), lambda i: (i, 0, 0))
    return pl.pallas_call(
        reorder_kernel,
        grid=(steps,),
        in_specs=[block],
        out_specs=block,
        out_shape=jax.ShapeDtypeStruct(bands.shape, bands.dtype),
        scratch_shapes=[pltpu.VMEM((depth, depth), jnp.bfloat16)],
        name="reorder_tiles",
    )(bands)


def parity_position(lane):
    within = lane % BS
    return 2 * (within % (BS // 2)) + within // (BS // 2)


def spread_matrix(offset):
    row = lax.broadcasted_iota(jnp.int32, (LANES, 2 * LANES), 0)
    col = lax.broadcasted_iota(jnp.int32, (LANES, 2 * LANES), 1)
    lane = col % LANES
    wanted_half = (col // LANES) == (lane // BS)
    hit = wanted_half & (row == parity_position(lane) + offset)
    return hit.astype(jnp.float32).astype(jnp.bfloat16)


def pack_blocks(index_ref, pick_at, low_ref, high_ref, out_ref):
    shards = out_ref.shape[0]
    for shard in range(shards):
        first = index_ref[pick_at + shard]
        second = index_ref[pick_at + shards + shard]
        out_ref[shard] = low_ref[first] + high_ref[second]


def pack_kernel(at, sources, index_hbm, in_ref, out_ref, index_ref, low_ref, high_ref, index_sem):
    tiles, rows = low_ref.shape[0] // 2, low_ref.shape[1]
    chunk = rows // sources
    index_copy = pltpu.make_async_copy(index_hbm.at[pl.ds(at * INDEX_STRIDE, INDEX_STRIDE)], index_ref, index_sem)
    index_copy.start()
    core = lax.axis_index("section") % 2
    for tile in range(tiles):
        span = pl.ds(tile * chunk, chunk)
        value = jnp.concatenate([in_ref[2 * source + core, span].astype(jnp.bfloat16) for source in range(sources)], axis=0)
        for offset in range(2):
            spread = jnp.dot(value, spread_matrix(offset * BS), preferred_element_type=jnp.float32).astype(jnp.bfloat16)
            low_ref[2 * tile + offset] = spread[:, :LANES]
            high_ref[2 * tile + offset] = spread[:, LANES:]
    index_copy.wait()
    pack_blocks(index_ref, PICKS_AT, low_ref, high_ref, out_ref)


def pack_rows(index, rows_in, at, sources, shards, rows, blocks):
    in_vmem = pl.BlockSpec(memory_space=pltpu.VMEM)
    return pl.pallas_call(
        functools.partial(pack_kernel, at, sources),
        in_specs=[pl.BlockSpec(memory_space=pl.ANY), in_vmem],
        out_specs=in_vmem,
        scratch_shapes=[
            pltpu.SMEM((INDEX_STRIDE,), jnp.int32),
            pltpu.VMEM((blocks, rows, LANES), jnp.bfloat16),
            pltpu.VMEM((blocks, rows, LANES), jnp.bfloat16),
            pltpu.SemaphoreType.DMA,
        ],
        out_shape=jax.ShapeDtypeStruct((shards, rows, LANES), jnp.bfloat16),
        compiler_params=pltpu.CompilerParams(vmem_limit_bytes=VMEM_LIMIT),
        name="pack_rows",
    )(index, rows_in)


def layer_kernel(layer, kind, index_hbm, in_ref, tiles_hbm, bias_ref, *refs):
    if kind == "first":
        sent_hbm, *refs = refs
    out_ref, index_ref, tiles_ref, spread_ref, total_ref, low_ref, high_ref, index_sem, tile_sems = refs
    shards, rows, _ = in_ref.shape
    groups = tiles_ref.shape[0]
    tile_slots = groups * GROUP
    blocks = total_ref.shape[1] - 1
    steps = tile_sems.shape[0]
    per_step = groups // steps
    index_copy = pltpu.make_async_copy(index_hbm.at[pl.ds(layer * INDEX_STRIDE, INDEX_STRIDE)], index_ref, index_sem)
    index_copy.start()
    def tile_copy(source, step):
        span = pl.ds(step * per_step, per_step)
        return pltpu.make_async_copy(source.at[span], tiles_ref.at[span], tile_sems.at[step])

    if kind == "first":
        core = lax.axis_index("section") % 2
        for step in range(steps):
            pl.when(core == 0)(tile_copy(tiles_hbm, step).start)
            pl.when(core == 1)(tile_copy(sent_hbm, step).start)
        tiles_of = tiles_hbm
    else:
        tiles_of = tiles_hbm.at[layer]
        for step in range(steps):
            tile_copy(tiles_of, step).start()
    total_ref[...] = jnp.zeros_like(total_ref)
    low = lax.broadcasted_iota(jnp.int32, (rows, LANES), 1) < BS
    for shard in range(shards):
        value = in_ref[shard].astype(jnp.float32)
        turned = pltpu.roll(value, BS, 1)
        spread_ref[0, 2 * shard] = jnp.where(low, value, 0.0).astype(jnp.bfloat16)
        spread_ref[0, 2 * shard + 1] = jnp.where(low, turned, 0.0).astype(jnp.bfloat16)
        spread_ref[1, 2 * shard] = jnp.where(low, 0.0, turned).astype(jnp.bfloat16)
        spread_ref[1, 2 * shard + 1] = jnp.where(low, 0.0, value).astype(jnp.bfloat16)
    index_copy.wait()
    empty = jnp.zeros((rows, LANES), jnp.bfloat16)
    for group in range(groups):
        if group % per_step == 0:
            tile_copy(tiles_of, group // per_step).wait()
        first_tile = group * GROUP
        left = []
        right = []
        for member in range(GROUP):
            pair = member // 2
            value = spread_ref[pair % 2, index_ref[first_tile + member]]
            left.append(value if pair < 2 else empty)
            right.append(value if pair >= 2 else empty)
        gathered = jnp.concatenate([jnp.concatenate(left, axis=0), jnp.concatenate(right, axis=0)], axis=1)
        product = jnp.dot(gathered, tiles_ref[group], preferred_element_type=jnp.float32)
        for member in range(GROUP):
            column = index_ref[tile_slots + first_tile + member]
            total_ref[member % 2, column] += product[member * rows : (member + 1) * rows]

    even = total_ref[0, :blocks].reshape(blocks * rows, LANES)
    odd = total_ref[1, :blocks].reshape(blocks * rows, LANES)
    summed = (even + pltpu.roll(odd, BS, 1)).reshape(blocks, rows, LANES) + bias_ref[layer][:, None, :]
    result = jnp.clip(summed, 0.0, CLAMP_TOP)
    if kind == "inner":
        value = jnp.dot(
            result.astype(jnp.bfloat16).reshape(blocks * rows, LANES),
            spread_matrix(0),
            preferred_element_type=jnp.float32,
        ).astype(jnp.bfloat16)
        low_ref[...] = value[:, :LANES].reshape(blocks, rows, LANES)
        high_ref[...] = value[:, LANES:].reshape(blocks, rows, LANES)
        pack_blocks(index_ref, PICKS_AT, low_ref, high_ref, out_ref)
        return
    low_rows = lax.broadcasted_iota(jnp.int32, (rows, LANES), 1) < BS
    for tile in range(blocks // 2):
        value = jnp.where(low_rows, result[2 * tile], pltpu.roll(result[2 * tile + 1], BS, 1)).astype(out_ref.dtype)
        if kind == "last":
            out_ref[:, tile * LANES : (tile + 1) * LANES] = value
        else:
            chunk = out_ref.shape[1] // (blocks // 2)
            for target in range(out_ref.shape[0]):
                at = target // 2 * chunk
                out_ref[target, tile * chunk : (tile + 1) * chunk] = value[at : at + chunk]


def run_layer(index, incoming, weights, bias, layer, kind, blocks, layers=None, sent=None):
    shards, rows, _ = incoming.shape
    groups, depth = weights.shape[-3:-1]
    steps = 4
    if kind == "first":
        out_shape = (layers, rows // (layers // 2) * blocks // 2, LANES)
    elif kind == "last":
        out_shape = (rows, blocks * BS)
    else:
        out_shape = (shards, rows, LANES)
    in_vmem = pl.BlockSpec(memory_space=pltpu.VMEM)
    anywhere = pl.BlockSpec(memory_space=pl.ANY)
    operands = [index, incoming, weights, bias] + ([sent] if kind == "first" else [])
    return pl.pallas_call(
        functools.partial(layer_kernel, layer, kind),
        in_specs=[anywhere, in_vmem, anywhere, in_vmem, anywhere][: len(operands)],
        out_specs=in_vmem,
        scratch_shapes=[
            pltpu.SMEM((INDEX_STRIDE,), jnp.int32),
            pltpu.VMEM((groups, depth, LANES), jnp.bfloat16),
            pltpu.VMEM((2, 2 * shards, rows, LANES), jnp.bfloat16),
            pltpu.VMEM((2, blocks + 1, rows, LANES), jnp.float32),
            pltpu.VMEM((blocks, rows, LANES), jnp.bfloat16),
            pltpu.VMEM((blocks, rows, LANES), jnp.bfloat16),
            pltpu.SemaphoreType.DMA,
            pltpu.SemaphoreType.DMA((steps,)),
        ],
        out_shape=jax.ShapeDtypeStruct(out_shape, jnp.bfloat16),
        compiler_params=pltpu.CompilerParams(vmem_limit_bytes=VMEM_LIMIT),
        cost_estimate=pl.CostEstimate(flops=2 * groups * GROUP * 2 * rows * depth * LANES, bytes_accessed=3 << 20, transcendentals=0),
        name="layer_step",
    )(*operands)


def plan_routes(tile_row, tile_col, tile_count, own_index, blocks_dev):
    shards = tile_count.shape[0]
    tile_slots = tile_col.shape[0]
    slot_ids = jnp.arange(tile_slots, dtype=jnp.int32)
    rows = tile_row.reshape(shards, tile_slots)
    own_rows = lax.dynamic_index_in_dim(rows, own_index, 0, keepdims=False)
    own_used = slot_ids < tile_count[own_index]
    own_shards = own_rows // blocks_dev
    earlier = (own_shards[None, :] == own_shards[:, None]) & (own_rows[None, :] < own_rows[:, None]) & own_used[None, :]
    rank = jnp.any(earlier, axis=1).astype(jnp.int32)
    slot = jnp.where(own_used, 2 * own_shards + rank, 0)
    column = jnp.where(own_used, tile_col, blocks_dev)
    wanted = (rows // blocks_dev == own_index) & (slot_ids[None, :] < tile_count[:, None])
    local = rows - own_index * blocks_dev
    lowest = jnp.min(jnp.where(wanted, local, blocks_dev - 1), axis=1)
    highest = jnp.max(jnp.where(wanted, local, 0), axis=1)
    return jnp.concatenate([slot, column, lowest, highest, jnp.zeros(INDEX_STRIDE - PICKS_AT - 2 * shards, jnp.int32)])


def body(features, tiles, tile_row, tile_col, tile_count, bias):
    shards = lax.axis_size("neuron")
    layers = lax.axis_size("section")
    own_index = lax.axis_index("neuron")
    rows, width = features.shape
    blocks = width // BS
    tile_slots = tiles.shape[1]
    with jax.named_scope("tile_order"):
        slabs = tiles[0].reshape(tile_slots // GROUP, GROUP, BS * BS // LANES, LANES)
        bands = slabs.transpose(0, 2, 1, 3).reshape(tile_slots // GROUP, GROUP * BS // 2, LANES)
        ordered = reorder_tiles(bands)
    with jax.named_scope("weight_gather"):
        weights = lax.all_gather(ordered, "section", axis=0)
    with jax.named_scope("routes"):
        routes = plan_routes(tile_row[0], tile_col[0], tile_count[0], own_index, blocks)
        tiled = features.astype(jnp.float32).reshape(rows, width // LANES, LANES).transpose(1, 0, 2).reshape(-1, LANES)
        own = jnp.concatenate([tiled, routes.astype(jnp.float32).reshape(-1, LANES), bias[0].reshape(width // LANES, LANES)])
        shared = lax.all_to_all(jnp.broadcast_to(own[None], (layers,) + own.shape), "section", 0, 0, tiled=True)
        index_at = tiled.shape[0]
        index_rows = INDEX_STRIDE // LANES
        pick_rows = PICKS_AT // LANES
        numbers = shared[:, index_at : index_at + index_rows].astype(jnp.int32)
        numbers = jnp.concatenate([numbers[:, :pick_rows], jnp.roll(numbers[:, pick_rows:], -1, axis=0)], axis=1)
        index = numbers.reshape(-1)
        biases = shared[:, index_at + index_rows :].reshape(layers, blocks, BS)
        biases = jnp.pad(biases, ((0, 0), (0, 0), (0, LANES - BS)))
    with jax.named_scope("first_layer"):
        sent = lax.ppermute(ordered, "section", [(source, source + 1) for source in range(0, layers, 2)])
        wide = rows * layers // 2
        outgoing = pack_rows(index, shared, layers - 1, layers // 2, shards, wide, blocks)
        incoming = lax.all_to_all(outgoing, "neuron", 0, 0, tiled=True)
        finished = run_layer(index, incoming, ordered, biases, 0, "first", blocks, layers, sent)
        spread_rows = lax.all_to_all(finished, "section", 0, 0, tiled=True)
    with jax.named_scope("layers"):
        outgoing = pack_rows(index, spread_rows, 0, 1, shards, rows, blocks)
        for layer in range(1, layers):
            incoming = lax.all_to_all(outgoing, "neuron", 0, 0, tiled=True)
            outgoing = run_layer(index, incoming, weights, biases, layer, "last" if layer == layers - 1 else "inner", blocks)
    return outgoing


def solution(mesh):
    in_specs = (
        P("section", "neuron"),
        P("section", "neuron", None),
        P("section", None),
        P("section", "neuron"),
        P("section", None),
        P("section", "neuron"),
    )
    out_specs = P("section", "neuron")
    return jax.shard_map(body, mesh=mesh, in_specs=in_specs, out_specs=out_specs, check_vma=False)
```

```python
import functools

import jax
import jax.numpy as jnp
from jax import lax
from jax.experimental import pallas as pl
from jax.experimental.pallas import tpu as pltpu
from jax.sharding import PartitionSpec as P

BS = 64
CLAMP_TOP = 32.0
LANES = 128
GROUP = 8
INDEX_STRIDE = 1024
PICKS_AT = 512
VMEM_LIMIT = 44 << 20


def reorder_kernel(in_ref, out_ref, move_ref):
    groups, depth, _ = in_ref.shape
    half = depth // GROUP
    pairs = GROUP // 2

    @pl.when(pl.program_id(0) == 0)
    def _():
        row = lax.broadcasted_iota(jnp.int32, (depth, depth), 0)
        col = lax.broadcasted_iota(jnp.int32, (depth, depth), 1)
        parity = row // (pairs * half)
        pair = row // half % pairs
        slab = row % half
        hit = col == slab * GROUP + 2 * pair + parity
        move_ref[...] = hit.astype(jnp.float32).astype(jnp.bfloat16)

    low = lax.broadcasted_iota(jnp.int32, (half, LANES), 1) < BS
    for group in range(groups):
        moved = jnp.dot(move_ref[...], in_ref[group], preferred_element_type=jnp.float32)
        for pair in range(pairs):
            first = moved[pair * half : (pair + 1) * half]
            second = moved[(pairs + pair) * half : (pairs + pair + 1) * half]
            even = jnp.where(low, first, pltpu.roll(second, BS, 1))
            odd = jnp.where(low, pltpu.roll(first, BS, 1), second)
            at = pair * 2 * half
            out_ref[group, at : at + half, :] = even.astype(out_ref.dtype)
            out_ref[group, at + half : at + 2 * half, :] = odd.astype(out_ref.dtype)


def reorder_tiles(bands):
    groups, depth, _ = bands.shape
    steps = 4
    block = pl.BlockSpec((groups // steps, depth, LANES), lambda i: (i, 0, 0))
    return pl.pallas_call(
        reorder_kernel,
        grid=(steps,),
        in_specs=[block],
        out_specs=block,
        out_shape=jax.ShapeDtypeStruct(bands.shape, bands.dtype),
        scratch_shapes=[pltpu.VMEM((depth, depth), jnp.bfloat16)],
        name="reorder_tiles",
    )(bands)


def parity_position(lane):
    within = lane % BS
    return 2 * (within % (BS // 2)) + within // (BS // 2)


def spread_matrix(offset):
    row = lax.broadcasted_iota(jnp.int32, (LANES, 2 * LANES), 0)
    col = lax.broadcasted_iota(jnp.int32, (LANES, 2 * LANES), 1)
    lane = col % LANES
    wanted_half = (col // LANES) == (lane // BS)
    hit = wanted_half & (row == parity_position(lane) + offset)
    return hit.astype(jnp.float32).astype(jnp.bfloat16)


def pack_blocks(index_ref, picks_at, low_ref, high_ref, out_ref):
    for shard in range(out_ref.shape[0]):
        first = index_ref[picks_at + 2 * shard]
        second = index_ref[picks_at + LANES + 2 * shard]
        out_ref[shard] = low_ref[first] + high_ref[second]


def pack_kernel(at, sources, index_hbm, in_ref, out_ref, index_ref, low_ref, high_ref, index_sem):
    chunk = out_ref.shape[1] // sources
    index_copy = pltpu.make_async_copy(index_hbm.at[pl.ds(at * INDEX_STRIDE, INDEX_STRIDE)], index_ref, index_sem)
    index_copy.start()
    core = lax.axis_index("section") % 2
    matrices = [spread_matrix(offset * BS) for offset in range(2)]
    for tile in range(low_ref.shape[0] // 2):
        span = pl.ds(tile * chunk, chunk)
        value = jnp.concatenate([in_ref[2 * source + core, span] for source in range(sources)], axis=0)
        for offset in range(2):
            spread = jnp.dot(value, matrices[offset], preferred_element_type=jnp.float32).astype(jnp.bfloat16)
            low_ref[2 * tile + offset] = spread[:, :LANES]
            high_ref[2 * tile + offset] = spread[:, LANES:]
    index_copy.wait()
    pack_blocks(index_ref, PICKS_AT, low_ref, high_ref, out_ref)


def pack_rows(index, rows_in, at, sources, shards, rows, blocks):
    in_vmem = pl.BlockSpec(memory_space=pltpu.VMEM)
    return pl.pallas_call(
        functools.partial(pack_kernel, at, sources),
        in_specs=[pl.BlockSpec(memory_space=pl.ANY), in_vmem],
        out_specs=in_vmem,
        scratch_shapes=[
            pltpu.SMEM((INDEX_STRIDE,), jnp.int32),
            pltpu.VMEM((blocks, rows, LANES), jnp.bfloat16),
            pltpu.VMEM((blocks, rows, LANES), jnp.bfloat16),
            pltpu.SemaphoreType.DMA,
        ],
        out_shape=jax.ShapeDtypeStruct((shards, rows, LANES), jnp.bfloat16),
        compiler_params=pltpu.CompilerParams(vmem_limit_bytes=VMEM_LIMIT),
        name="pack_rows",
    )(index, rows_in)


def layer_kernel(layer, kind, fetch, ahead, *refs):
    refs = list(refs)
    index_hbm, in_ref, bias_ref = (refs.pop(0) for _ in range(3))
    given_ref = None if fetch else refs.pop(0)
    sent_hbm = refs.pop(0) if kind == "first" else None
    weights_hbm = refs.pop(0) if fetch or ahead else None
    out_ref = refs.pop(0)
    next_ref = refs.pop(0) if ahead else None
    index_ref, fetched_ref, spread_ref, low_ref, high_ref, index_sem, tile_sems, next_sem, *total_refs = refs
    tiles_ref = fetched_ref if fetch else given_ref
    shards, rows, _ = in_ref.shape
    groups = tiles_ref.shape[0]
    tile_slots = groups * GROUP
    blocks = total_refs[0].shape[0] - 1
    steps = tile_sems.shape[0]
    per_step = groups // steps
    index_copy = pltpu.make_async_copy(
        index_hbm.at[pl.ds(layer * INDEX_STRIDE, index_ref.shape[0])], index_ref, index_sem
    )
    index_copy.start()

    def tile_copy(source, step):
        span = pl.ds(step * per_step, per_step)
        return pltpu.make_async_copy(source.at[span], fetched_ref.at[span], tile_sems.at[step])

    if kind == "first":
        core = lax.axis_index("section") % 2
        tiles_hbm = weights_hbm
        for step in range(steps):
            pl.when(core == 0)(tile_copy(tiles_hbm, step).start)
            pl.when(core == 1)(tile_copy(sent_hbm, step).start)
    elif fetch:
        tiles_hbm = weights_hbm.at[layer]
        for step in range(steps):
            tile_copy(tiles_hbm, step).start()
    if ahead:
        next_copy = pltpu.make_async_copy(weights_hbm.at[layer + 1], next_ref, next_sem)
        next_copy.start()
    for total_ref in total_refs:
        total_ref[...] = jnp.zeros_like(total_ref)
    low = lax.broadcasted_iota(jnp.int32, (rows, LANES), 1) < BS
    for shard in range(shards):
        value = in_ref[shard].astype(jnp.float32)
        turned = pltpu.roll(value, BS, 1)
        spread_ref[0, 2 * shard] = jnp.where(low, value, 0.0).astype(jnp.bfloat16)
        spread_ref[0, 2 * shard + 1] = jnp.where(low, turned, 0.0).astype(jnp.bfloat16)
        spread_ref[1, 2 * shard] = jnp.where(low, 0.0, turned).astype(jnp.bfloat16)
        spread_ref[1, 2 * shard + 1] = jnp.where(low, 0.0, value).astype(jnp.bfloat16)
    index_copy.wait()
    empty = jnp.zeros((rows, LANES), jnp.bfloat16)
    for group in range(groups):
        if fetch and group % per_step == 0:
            tile_copy(tiles_hbm, group // per_step).wait()
        first_tile = group * GROUP
        left = []
        right = []
        for member in range(GROUP):
            pair = member // 2
            value = spread_ref[pair % 2, index_ref[first_tile + member]]
            left.append(value if pair < 2 else empty)
            right.append(value if pair >= 2 else empty)
        gathered = jnp.concatenate([jnp.concatenate(left, axis=0), jnp.concatenate(right, axis=0)], axis=1)
        product = jnp.dot(gathered, tiles_ref[group], preferred_element_type=jnp.float32)
        for member in range(GROUP):
            column = index_ref[tile_slots + first_tile + member]
            total_refs[member][column] += product[member * rows : (member + 1) * rows]

    even, odd = (
        sum(total_refs[member][:blocks] for member in range(parity, GROUP, 2)).reshape(blocks * rows, LANES)
        for parity in range(2)
    )
    summed = (even + pltpu.roll(odd, BS, 1)).reshape(blocks, rows, LANES) + bias_ref[layer][:, None, :]
    result = jnp.clip(summed, 0.0, CLAMP_TOP)
    if kind == "inner":
        value = jnp.dot(
            result.astype(jnp.bfloat16).reshape(blocks * rows, LANES),
            spread_matrix(0),
            preferred_element_type=jnp.float32,
        ).astype(jnp.bfloat16)
        low_ref[...] = value[:, :LANES].reshape(blocks, rows, LANES)
        high_ref[...] = value[:, LANES:].reshape(blocks, rows, LANES)
        pack_blocks(index_ref, INDEX_STRIDE + PICKS_AT, low_ref, high_ref, out_ref)
        if ahead:
            next_copy.wait()
        return
    low_rows = lax.broadcasted_iota(jnp.int32, (rows, LANES), 1) < BS
    for tile in range(blocks // 2):
        value = jnp.where(low_rows, result[2 * tile], pltpu.roll(result[2 * tile + 1], BS, 1)).astype(out_ref.dtype)
        if kind == "last":
            out_ref[:, tile * LANES : (tile + 1) * LANES] = value
        else:
            chunk = out_ref.shape[1] // (blocks // 2)
            for target in range(out_ref.shape[0]):
                at = target // 2 * chunk
                out_ref[target, tile * chunk : (tile + 1) * chunk] = value[at : at + chunk]


def run_layer(index, incoming, bias, layer, kind, blocks, layers, weights=None, given=None, sent=None):
    shards, rows, _ = incoming.shape
    fetch = given is None
    ahead = kind == "inner"
    groups, depth = (weights if fetch else given).shape[-3:-1]
    steps = 4
    if kind == "first":
        out_shape = (layers, rows // (layers // 2) * blocks // 2, LANES)
    elif kind == "last":
        out_shape = (rows, blocks * BS)
    else:
        out_shape = (shards, rows, LANES)
    in_vmem = pl.BlockSpec(memory_space=pltpu.VMEM)
    anywhere = pl.BlockSpec(memory_space=pl.ANY)
    operands = [(index, anywhere), (incoming, in_vmem), (bias, in_vmem)]
    if not fetch:
        operands.append((given, in_vmem))
    if kind == "first":
        operands.append((sent, anywhere))
    if fetch or ahead:
        operands.append((weights, anywhere))
    results = [jax.ShapeDtypeStruct(out_shape, jnp.bfloat16)]
    if ahead:
        results.append(jax.ShapeDtypeStruct((groups, depth, LANES), jnp.bfloat16))
    done = pl.pallas_call(
        functools.partial(layer_kernel, layer, kind, fetch, ahead),
        in_specs=[spec for _, spec in operands],
        out_specs=[in_vmem] * len(results),
        scratch_shapes=[
            pltpu.SMEM((2 * INDEX_STRIDE if kind == "inner" else INDEX_STRIDE,), jnp.int32),
            pltpu.VMEM((groups if fetch else 1, depth, LANES), jnp.bfloat16),
            pltpu.VMEM((2, 2 * shards, rows, LANES), jnp.bfloat16),
            pltpu.VMEM((blocks, rows, LANES), jnp.bfloat16),
            pltpu.VMEM((blocks, rows, LANES), jnp.bfloat16),
            pltpu.SemaphoreType.DMA,
            pltpu.SemaphoreType.DMA((steps,)),
            pltpu.SemaphoreType.DMA,
        ]
        + [pltpu.VMEM((blocks + 1, rows, LANES), jnp.float32)] * GROUP,
        out_shape=results,
        compiler_params=pltpu.CompilerParams(vmem_limit_bytes=VMEM_LIMIT),
        cost_estimate=pl.CostEstimate(flops=2 * groups * GROUP * 2 * rows * depth * LANES, bytes_accessed=3 << 20, transcendentals=0),
        name="layer_step",
    )(*[operand for operand, _ in operands])
    return done if ahead else done[0]


def plan_kernel(blocks_dev, count_ref, rows_ref, cols_ref, counts_ref, bias_ref, in_ref, out_ref):
    own = lax.axis_index("neuron")
    per_shard = cols_ref.shape[0]
    lane = lax.broadcasted_iota(jnp.int32, (LANES, LANES), 1)
    sub = lax.broadcasted_iota(jnp.int32, (LANES, LANES), 0)
    unused = 1 << 16
    own_rows = rows_ref[pl.ds(own * per_shard, per_shard), :]
    slot_ids = lax.broadcasted_iota(jnp.int32, (per_shard, LANES), 0) * LANES + lax.broadcasted_iota(
        jnp.int32, (per_shard, LANES), 1
    )
    used = slot_ids < count_ref[own]
    known = jnp.where(used, own_rows, unused)
    across = [jnp.broadcast_to(own_rows[half : half + 1], (LANES, LANES)) for half in range(per_shard)]
    down = [
        jnp.broadcast_to(known[half : half + 1].astype(jnp.float32), (LANES, LANES)).T.astype(jnp.int32)
        for half in range(per_shard)
    ]
    ranks = []
    for here in across:
        earlier = jnp.zeros((1, LANES), jnp.int32)
        for there in down:
            hit = (there // blocks_dev == here // blocks_dev) & (there < here)
            earlier = jnp.maximum(earlier, jnp.max(hit.astype(jnp.int32), axis=0, keepdims=True))
        ranks.append(earlier)
    rank = jnp.concatenate(ranks, axis=0)
    slot = jnp.where(used, 2 * (own_rows // blocks_dev) + rank, 0)
    column = jnp.where(used, cols_ref[...], blocks_dev)
    counts = jnp.sum(
        jnp.where(lane == sub // per_shard, jnp.broadcast_to(counts_ref[...], (LANES, LANES)), 0).astype(jnp.float32),
        axis=1,
        keepdims=True,
    ).astype(jnp.int32)
    rows = rows_ref[...]
    wanted = (rows // blocks_dev == own) & ((sub % per_shard) * LANES + lane < counts)
    local = rows - own * blocks_dev
    lowest = jnp.min(jnp.where(wanted, local, blocks_dev - 1).astype(jnp.float32), axis=1, keepdims=True)
    highest = jnp.max(jnp.where(wanted, local, 0).astype(jnp.float32), axis=1, keepdims=True)
    lowest = jnp.broadcast_to(lowest, (LANES, LANES)).T[:8]
    highest = jnp.broadcast_to(highest, (LANES, LANES)).T[:8]
    lowest = jnp.minimum(lowest, pltpu.roll(lowest, LANES - 1, 1))
    highest = jnp.maximum(highest, pltpu.roll(highest, LANES - 1, 1))
    numbers = [slot.astype(jnp.float32), column.astype(jnp.float32), lowest[:1], highest[:1]]
    numbers.append(jnp.zeros((14 - 2 * per_shard, LANES), jnp.float32))
    bias = bias_ref[...]
    rounded = bias.astype(jnp.bfloat16)
    rest = bias - rounded.astype(jnp.float32)
    rest_rounded = rest.astype(jnp.bfloat16)
    last = (rest - rest_rounded.astype(jnp.float32)).astype(jnp.bfloat16)
    small = jnp.concatenate(numbers, axis=0).astype(jnp.bfloat16)
    parts = jnp.concatenate([rounded.astype(jnp.float32), rest_rounded.astype(jnp.float32)], axis=0).astype(jnp.bfloat16)
    ends = jnp.concatenate([last.astype(jnp.float32), jnp.zeros_like(bias)], axis=0).astype(jnp.bfloat16)
    rows_in, width = in_ref.shape
    for target in range(out_ref.shape[0]):
        for tile in range(width // LANES):
            out_ref[target, tile * rows_in : (tile + 1) * rows_in] = in_ref[:, tile * LANES : (tile + 1) * LANES]
        at = rows_in * width // LANES
        for piece in (small, parts, ends):
            out_ref[target, at : at + piece.shape[0]] = piece
            at += piece.shape[0]


def plan_routes(tile_row, tile_col, tile_count, bias, features, blocks_dev, layers):
    shards = tile_count.shape[1]
    rows, width = features.shape
    in_vmem = pl.BlockSpec(memory_space=pltpu.VMEM)
    counts = jnp.pad(tile_count, ((0, 0), (0, LANES - shards)))
    return pl.pallas_call(
        functools.partial(plan_kernel, blocks_dev),
        in_specs=[pl.BlockSpec(memory_space=pltpu.SMEM)] + [in_vmem] * 5,
        out_specs=in_vmem,
        out_shape=jax.ShapeDtypeStruct((layers, rows * width // LANES + 48, LANES), jnp.bfloat16),
        cost_estimate=pl.CostEstimate(flops=0, bytes_accessed=4 << 20, transcendentals=0),
        name="plan_routes",
    )(
        tile_count[0],
        tile_row.reshape(-1, LANES),
        tile_col.reshape(-1, LANES),
        counts,
        bias.reshape(-1, LANES),
        features,
    )


def body(features, tiles, tile_row, tile_col, tile_count, bias):
    shards = lax.axis_size("neuron")
    layers = lax.axis_size("section")
    rows, width = features.shape
    blocks = width // BS
    tile_slots = tiles.shape[1]
    to_odd = [(source, source + 1) for source in range(0, layers, 2)]
    with jax.named_scope("tile_order"):
        slabs = tiles[0].reshape(tile_slots // GROUP, GROUP, BS * BS // LANES, LANES)
        bands = slabs.transpose(0, 2, 1, 3).reshape(tile_slots // GROUP, GROUP * BS // 2, LANES)
        ordered = reorder_tiles(bands)
    with jax.named_scope("weight_gather"):
        weights = lax.all_gather(ordered, "section", axis=0)
    with jax.named_scope("routes"):
        plan = plan_routes(tile_row, tile_col, tile_count, bias, features, blocks, layers)
        shared = lax.all_to_all(plan, "section", 0, 0, tiled=True)
        at = rows * width // LANES
        index = shared[:, at : at + 8].astype(jnp.int32).reshape(-1)
        parts = [shared[:, at + start : at + start + 8].astype(jnp.float32) for start in (16, 24, 32)]
        biases = (parts[0] + parts[1] + parts[2]).reshape(layers, blocks, BS)
        biases = jnp.pad(biases, ((0, 0), (0, 0), (0, LANES - BS)))
    with jax.named_scope("first_layer"):
        sent = lax.ppermute(ordered, "section", to_odd)
        outgoing = pack_rows(index, shared, 0, layers // 2, shards, rows * layers // 2, blocks)
        incoming = lax.all_to_all(outgoing, "neuron", 0, 0, tiled=True)
        finished = run_layer(index, incoming, biases, 0, "first", blocks, layers, weights=ordered, sent=sent)
        own_rows = lax.all_to_all(finished, "section", 0, 0, tiled=True)
    with jax.named_scope("layers"):
        outgoing = pack_rows(index, own_rows, 1, 1, shards, rows, blocks)
        given = None
        for layer in range(1, layers - 1):
            incoming = lax.all_to_all(outgoing, "neuron", 0, 0, tiled=True)
            outgoing, given = run_layer(index, incoming, biases, layer, "inner", blocks, layers, weights, given)
        incoming = lax.all_to_all(outgoing, "neuron", 0, 0, tiled=True)
        return run_layer(index, incoming, biases, layers - 1, "last", blocks, layers, given=given)


def solution(mesh):
    in_specs = (
        P("section", "neuron"),
        P("section", "neuron", None),
        P("section", None),
        P("section", "neuron"),
        P("section", None),
        P("section", "neuron"),
    )
    out_specs = P("section", "neuron")
    return jax.shard_map(body, mesh=mesh, in_specs=in_specs, out_specs=out_specs, check_vma=False)
```

```python
import functools

import jax
import jax.numpy as jnp
from jax import lax
from jax.experimental import pallas as pl
from jax.experimental.pallas import tpu as pltpu
from jax.sharding import PartitionSpec as P

BS = 64
CLAMP_TOP = 32.0
LANES = 128
GROUP = 8
INDEX_STRIDE = 1024
PICKS_AT = 512
VMEM_LIMIT = 44 << 20


def reorder_kernel(in_hbm, out_hbm, in_ref, out_ref, in_sems, out_sems):
    groups, depth, _ = in_ref.shape
    half = depth // GROUP
    pairs = GROUP // 2
    steps = in_sems.shape[0]
    per_step = groups // steps
    spans = [pl.ds(step * per_step, per_step) for step in range(steps)]
    arrivals = [pltpu.make_async_copy(in_hbm.at[span], in_ref.at[span], in_sems.at[step]) for step, span in enumerate(spans)]
    leaves = [pltpu.make_async_copy(out_ref.at[span], out_hbm.at[span], out_sems.at[step]) for step, span in enumerate(spans)]
    for copy in arrivals:
        copy.start()
    row = lax.broadcasted_iota(jnp.int32, (depth, depth), 0)
    col = lax.broadcasted_iota(jnp.int32, (depth, depth), 1)
    parity = row // (pairs * half)
    pair = row // half % pairs
    slab = row % half
    move = (col == slab * GROUP + 2 * pair + parity).astype(jnp.float32).astype(jnp.bfloat16)
    low = lax.broadcasted_iota(jnp.int32, (half, LANES), 1) < BS
    for step in range(steps):
        arrivals[step].wait()
        for group in range(step * per_step, (step + 1) * per_step):
            moved = jnp.dot(move, in_ref[group], preferred_element_type=jnp.float32)
            for pair in range(pairs):
                first = moved[pair * half : (pair + 1) * half]
                second = moved[(pairs + pair) * half : (pairs + pair + 1) * half]
                even = jnp.where(low, first, pltpu.roll(second, BS, 1))
                odd = jnp.where(low, pltpu.roll(first, BS, 1), second)
                at = pair * 2 * half
                out_ref[group, at : at + half, :] = even.astype(out_ref.dtype)
                out_ref[group, at + half : at + 2 * half, :] = odd.astype(out_ref.dtype)
        leaves[step].start()
    for copy in leaves:
        copy.wait()


def reorder_tiles(bands):
    steps = 4
    anywhere = pl.BlockSpec(memory_space=pl.ANY)
    return pl.pallas_call(
        reorder_kernel,
        in_specs=[anywhere],
        out_specs=anywhere,
        out_shape=jax.ShapeDtypeStruct(bands.shape, bands.dtype),
        scratch_shapes=[
            pltpu.VMEM(bands.shape, bands.dtype),
            pltpu.VMEM(bands.shape, bands.dtype),
            pltpu.SemaphoreType.DMA((steps,)),
            pltpu.SemaphoreType.DMA((steps,)),
        ],
        compiler_params=pltpu.CompilerParams(vmem_limit_bytes=62 << 20),
        name="reorder_tiles",
    )(bands)


def parity_position(lane):
    within = lane % BS
    return 2 * (within % (BS // 2)) + within // (BS // 2)


def spread_matrix(offset):
    row = lax.broadcasted_iota(jnp.int32, (LANES, 2 * LANES), 0)
    col = lax.broadcasted_iota(jnp.int32, (LANES, 2 * LANES), 1)
    lane = col % LANES
    wanted_half = (col // LANES) == (lane // BS)
    hit = wanted_half & (row == parity_position(lane) + offset)
    return hit.astype(jnp.float32).astype(jnp.bfloat16)


def pack_blocks(index_ref, picks_at, low_ref, high_ref, out_ref):
    for shard in range(out_ref.shape[0]):
        first = index_ref[picks_at + 2 * shard]
        second = index_ref[picks_at + LANES + 2 * shard]
        out_ref[shard] = low_ref[first] + high_ref[second]


def pack_kernel(at, sources, index_hbm, in_ref, out_ref, index_ref, low_ref, high_ref, index_sem):
    chunk = out_ref.shape[1] // sources
    index_copy = pltpu.make_async_copy(index_hbm.at[pl.ds(at * INDEX_STRIDE, INDEX_STRIDE)], index_ref, index_sem)
    index_copy.start()
    core = lax.axis_index("section") % 2
    matrices = [spread_matrix(offset * BS) for offset in range(2)]
    for tile in range(low_ref.shape[0] // 2):
        span = pl.ds(tile * chunk, chunk)
        value = jnp.concatenate([in_ref[2 * source + core, span] for source in range(sources)], axis=0)
        for offset in range(2):
            spread = jnp.dot(value, matrices[offset], preferred_element_type=jnp.float32).astype(jnp.bfloat16)
            low_ref[2 * tile + offset] = spread[:, :LANES]
            high_ref[2 * tile + offset] = spread[:, LANES:]
    index_copy.wait()
    pack_blocks(index_ref, PICKS_AT, low_ref, high_ref, out_ref)


def pack_rows(index, rows_in, at, sources, shards, rows, blocks):
    in_vmem = pl.BlockSpec(memory_space=pltpu.VMEM)
    return pl.pallas_call(
        functools.partial(pack_kernel, at, sources),
        in_specs=[pl.BlockSpec(memory_space=pl.ANY), in_vmem],
        out_specs=in_vmem,
        scratch_shapes=[
            pltpu.SMEM((INDEX_STRIDE,), jnp.int32),
            pltpu.VMEM((blocks, rows, LANES), jnp.bfloat16),
            pltpu.VMEM((blocks, rows, LANES), jnp.bfloat16),
            pltpu.SemaphoreType.DMA,
        ],
        out_shape=jax.ShapeDtypeStruct((shards, rows, LANES), jnp.bfloat16),
        compiler_params=pltpu.CompilerParams(vmem_limit_bytes=VMEM_LIMIT),
        name="pack_rows",
    )(index, rows_in)


def layer_kernel(layer, kind, fetch, ahead, *refs):
    refs = list(refs)
    index_hbm, in_ref, bias_ref = (refs.pop(0) for _ in range(3))
    given_ref = None if fetch else refs.pop(0)
    weights_hbm = refs.pop(0) if fetch or ahead else None
    out_ref = refs.pop(0)
    next_ref = refs.pop(0) if ahead else None
    index_ref, fetched_ref, spread_ref, low_ref, high_ref, index_sem, tile_sems, next_sem, *total_refs = refs
    tiles_ref = fetched_ref if fetch else given_ref
    shards, rows, _ = in_ref.shape
    groups = tiles_ref.shape[0]
    tile_slots = groups * GROUP
    blocks = total_refs[0].shape[0] - 1
    steps = tile_sems.shape[0]
    per_step = groups // steps
    index_copy = pltpu.make_async_copy(
        index_hbm.at[pl.ds(layer * INDEX_STRIDE, index_ref.shape[0])], index_ref, index_sem
    )
    index_copy.start()

    def tile_copy(source, step):
        span = pl.ds(step * per_step, per_step)
        return pltpu.make_async_copy(source.at[span], fetched_ref.at[span], tile_sems.at[step])

    if fetch:
        tiles_hbm = weights_hbm.at[layer]
        for step in range(steps):
            tile_copy(tiles_hbm, step).start()
    if ahead:
        next_copy = pltpu.make_async_copy(weights_hbm.at[layer + 1], next_ref, next_sem)
        next_copy.start()
    for total_ref in total_refs:
        total_ref[...] = jnp.zeros_like(total_ref)
    low = lax.broadcasted_iota(jnp.int32, (rows, LANES), 1) < BS
    for shard in range(shards):
        value = in_ref[shard].astype(jnp.float32)
        turned = pltpu.roll(value, BS, 1)
        spread_ref[0, 2 * shard] = jnp.where(low, value, 0.0).astype(jnp.bfloat16)
        spread_ref[0, 2 * shard + 1] = jnp.where(low, turned, 0.0).astype(jnp.bfloat16)
        spread_ref[1, 2 * shard] = jnp.where(low, 0.0, turned).astype(jnp.bfloat16)
        spread_ref[1, 2 * shard + 1] = jnp.where(low, 0.0, value).astype(jnp.bfloat16)
    index_copy.wait()
    empty = jnp.zeros((rows, LANES), jnp.bfloat16)
    for group in range(groups):
        if fetch and group % per_step == 0:
            tile_copy(tiles_hbm, group // per_step).wait()
        first_tile = group * GROUP
        left = []
        right = []
        for member in range(GROUP):
            pair = member // 2
            value = spread_ref[pair % 2, index_ref[first_tile + member]]
            left.append(value if pair < 2 else empty)
            right.append(value if pair >= 2 else empty)
        gathered = jnp.concatenate([jnp.concatenate(left, axis=0), jnp.concatenate(right, axis=0)], axis=1)
        product = jnp.dot(gathered, tiles_ref[group], preferred_element_type=jnp.float32)
        for member in range(GROUP):
            column = index_ref[tile_slots + first_tile + member]
            total_refs[member][column] += product[member * rows : (member + 1) * rows]

    even, odd = (
        sum(total_refs[member][:blocks] for member in range(parity, GROUP, 2)).reshape(blocks * rows, LANES)
        for parity in range(2)
    )
    summed = (even + pltpu.roll(odd, BS, 1)).reshape(blocks, rows, LANES) + bias_ref[layer][:, None, :]
    result = jnp.clip(summed, 0.0, CLAMP_TOP)
    if kind == "inner":
        value = jnp.dot(
            result.astype(jnp.bfloat16).reshape(blocks * rows, LANES),
            spread_matrix(0),
            preferred_element_type=jnp.float32,
        ).astype(jnp.bfloat16)
        low_ref[...] = value[:, :LANES].reshape(blocks, rows, LANES)
        high_ref[...] = value[:, LANES:].reshape(blocks, rows, LANES)
        pack_blocks(index_ref, INDEX_STRIDE + PICKS_AT, low_ref, high_ref, out_ref)
        if ahead:
            next_copy.wait()
        return
    low_rows = lax.broadcasted_iota(jnp.int32, (rows, LANES), 1) < BS
    for tile in range(blocks // 2):
        value = jnp.where(low_rows, result[2 * tile], pltpu.roll(result[2 * tile + 1], BS, 1)).astype(out_ref.dtype)
        if kind == "last":
            out_ref[:, tile * LANES : (tile + 1) * LANES] = value
        else:
            chunk = out_ref.shape[1] // (blocks // 2)
            for target in range(out_ref.shape[0]):
                at = target // 2 * chunk
                out_ref[target, tile * chunk : (tile + 1) * chunk] = value[at : at + chunk]


def run_layer(index, incoming, bias, layer, kind, blocks, layers, weights=None, given=None):
    shards, rows, _ = incoming.shape
    fetch = given is None
    ahead = kind == "inner"
    groups, depth = (weights if fetch else given).shape[-3:-1]
    steps = 2
    if kind == "first":
        out_shape = (layers, rows // (layers // 2) * blocks // 2, LANES)
    elif kind == "last":
        out_shape = (rows, blocks * BS)
    else:
        out_shape = (shards, rows, LANES)
    in_vmem = pl.BlockSpec(memory_space=pltpu.VMEM)
    anywhere = pl.BlockSpec(memory_space=pl.ANY)
    operands = [(index, anywhere), (incoming, in_vmem), (bias, in_vmem)]
    if not fetch:
        operands.append((given, in_vmem))
    if fetch or ahead:
        operands.append((weights, anywhere))
    results = [jax.ShapeDtypeStruct(out_shape, jnp.bfloat16)]
    if ahead:
        results.append(jax.ShapeDtypeStruct((groups, depth, LANES), jnp.bfloat16))
    done = pl.pallas_call(
        functools.partial(layer_kernel, layer, kind, fetch, ahead),
        in_specs=[spec for _, spec in operands],
        out_specs=[in_vmem] * len(results),
        scratch_shapes=[
            pltpu.SMEM((2 * INDEX_STRIDE if kind == "inner" else INDEX_STRIDE,), jnp.int32),
            pltpu.VMEM((groups if fetch else 1, depth, LANES), jnp.bfloat16),
            pltpu.VMEM((2, 2 * shards, rows, LANES), jnp.bfloat16),
            pltpu.VMEM((blocks, rows, LANES), jnp.bfloat16),
            pltpu.VMEM((blocks, rows, LANES), jnp.bfloat16),
            pltpu.SemaphoreType.DMA,
            pltpu.SemaphoreType.DMA((steps,)),
            pltpu.SemaphoreType.DMA,
        ]
        + [pltpu.VMEM((blocks + 1, rows, LANES), jnp.float32)] * GROUP,
        out_shape=results,
        compiler_params=pltpu.CompilerParams(vmem_limit_bytes=VMEM_LIMIT),
        cost_estimate=pl.CostEstimate(flops=2 * groups * GROUP * 2 * rows * depth * LANES, bytes_accessed=3 << 20, transcendentals=0),
        name="layer_step",
    )(*[operand for operand, _ in operands])
    return done if ahead else done[0]


def plan_kernel(blocks_dev, count_ref, rows_ref, cols_ref, counts_ref, bias_ref, in_ref, out_ref):
    own = lax.axis_index("neuron")
    per_shard = cols_ref.shape[0]
    lane = lax.broadcasted_iota(jnp.int32, (LANES, LANES), 1)
    sub = lax.broadcasted_iota(jnp.int32, (LANES, LANES), 0)
    unused = 1 << 16
    own_rows = rows_ref[pl.ds(own * per_shard, per_shard), :]
    slot_ids = lax.broadcasted_iota(jnp.int32, (per_shard, LANES), 0) * LANES + lax.broadcasted_iota(
        jnp.int32, (per_shard, LANES), 1
    )
    used = slot_ids < count_ref[own]
    known = jnp.where(used, own_rows, unused)
    across = [jnp.broadcast_to(own_rows[half : half + 1], (LANES, LANES)) for half in range(per_shard)]
    down = [
        jnp.broadcast_to(known[half : half + 1].astype(jnp.float32), (LANES, LANES)).T.astype(jnp.int32)
        for half in range(per_shard)
    ]
    ranks = []
    for here in across:
        earlier = jnp.zeros((1, LANES), jnp.int32)
        for there in down:
            hit = (there // blocks_dev == here // blocks_dev) & (there < here)
            earlier = jnp.maximum(earlier, jnp.max(hit.astype(jnp.int32), axis=0, keepdims=True))
        ranks.append(earlier)
    rank = jnp.concatenate(ranks, axis=0)
    slot = jnp.where(used, 2 * (own_rows // blocks_dev) + rank, 0)
    column = jnp.where(used, cols_ref[...], blocks_dev)
    shards = counts_ref.shape[1]
    shard_lane = lax.broadcasted_iota(jnp.int32, (LANES, shards), 1)
    shard_sub = lax.broadcasted_iota(jnp.int32, (LANES, shards), 0) // per_shard
    counts = jnp.sum(
        jnp.where(shard_lane == shard_sub, jnp.broadcast_to(counts_ref[...], (LANES, shards)), 0).astype(jnp.float32),
        axis=1,
        keepdims=True,
    ).astype(jnp.int32)
    rows = rows_ref[...]
    wanted = (rows // blocks_dev == own) & ((sub % per_shard) * LANES + lane < counts)
    local = rows - own * blocks_dev
    lowest = jnp.min(jnp.where(wanted, local, blocks_dev - 1).astype(jnp.float32), axis=1, keepdims=True)
    highest = jnp.max(jnp.where(wanted, local, 0).astype(jnp.float32), axis=1, keepdims=True)
    lowest = jnp.broadcast_to(lowest, (LANES, LANES)).T[:8]
    highest = jnp.broadcast_to(highest, (LANES, LANES)).T[:8]
    lowest = jnp.minimum(lowest, pltpu.roll(lowest, LANES - 1, 1))
    highest = jnp.maximum(highest, pltpu.roll(highest, LANES - 1, 1))
    numbers = [slot.astype(jnp.float32), column.astype(jnp.float32), lowest[:1], highest[:1]]
    numbers.append(jnp.zeros((14 - 2 * per_shard, LANES), jnp.float32))
    bias = bias_ref[...]
    rounded = bias.astype(jnp.bfloat16)
    rest = bias - rounded.astype(jnp.float32)
    rest_rounded = rest.astype(jnp.bfloat16)
    last = (rest - rest_rounded.astype(jnp.float32)).astype(jnp.bfloat16)
    small = jnp.concatenate(numbers, axis=0).astype(jnp.bfloat16)
    parts = jnp.concatenate([rounded.astype(jnp.float32), rest_rounded.astype(jnp.float32)], axis=0).astype(jnp.bfloat16)
    ends = jnp.concatenate([last.astype(jnp.float32), jnp.zeros_like(bias)], axis=0).astype(jnp.bfloat16)
    rows_in, width = in_ref.shape
    for target in range(out_ref.shape[0]):
        for tile in range(width // LANES):
            out_ref[target, tile * rows_in : (tile + 1) * rows_in] = in_ref[:, tile * LANES : (tile + 1) * LANES]
        at = rows_in * width // LANES
        for piece in (small, parts, ends):
            out_ref[target, at : at + piece.shape[0]] = piece
            at += piece.shape[0]


def plan_routes(tile_row, tile_col, tile_count, bias, features, blocks_dev, layers):
    rows, width = features.shape
    in_vmem = pl.BlockSpec(memory_space=pltpu.VMEM)
    return pl.pallas_call(
        functools.partial(plan_kernel, blocks_dev),
        in_specs=[pl.BlockSpec(memory_space=pltpu.SMEM)] + [in_vmem] * 5,
        out_specs=in_vmem,
        out_shape=jax.ShapeDtypeStruct((layers, rows * width // LANES + 48, LANES), jnp.bfloat16),
        cost_estimate=pl.CostEstimate(flops=0, bytes_accessed=4 << 20, transcendentals=0),
        name="plan_routes",
    )(
        tile_count[0],
        tile_row.reshape(-1, LANES),
        tile_col.reshape(-1, LANES),
        tile_count,
        bias.reshape(-1, LANES),
        features,
    )


def body(features, tiles, tile_row, tile_col, tile_count, bias):
    shards = lax.axis_size("neuron")
    layers = lax.axis_size("section")
    rows, width = features.shape
    blocks = width // BS
    tile_slots = tiles.shape[1]
    to_odd = [(source, source + 1) for source in range(0, layers, 2)]
    with jax.named_scope("tile_order"):
        slabs = tiles[0].reshape(tile_slots // GROUP, GROUP, BS * BS // LANES, LANES)
        bands = slabs.transpose(0, 2, 1, 3).reshape(tile_slots // GROUP, GROUP * BS // 2, LANES)
        ordered = reorder_tiles(bands)
    with jax.named_scope("weight_gather"):
        weights = lax.all_gather(ordered, "section", axis=0)
    with jax.named_scope("routes"):
        plan = plan_routes(tile_row, tile_col, tile_count, bias, features, blocks, layers)
        shared = lax.all_to_all(plan, "section", 0, 0, tiled=True)
        at = rows * width // LANES
        index = shared[:, at : at + 8].astype(jnp.int32).reshape(-1)
        parts = [shared[:, at + start : at + start + 8].astype(jnp.float32) for start in (16, 24, 32)]
        biases = (parts[0] + parts[1] + parts[2]).reshape(layers, blocks, BS)
        biases = jnp.pad(biases, ((0, 0), (0, 0), (0, LANES - BS)))
    with jax.named_scope("first_layer"):
        sent = lax.ppermute(ordered, "section", to_odd)
        first_tiles = jnp.where(lax.axis_index("section") % 2 == 0, ordered, sent)
        outgoing = pack_rows(index, shared, 0, layers // 2, shards, rows * layers // 2, blocks)
        incoming = lax.all_to_all(outgoing, "neuron", 0, 0, tiled=True)
        finished = run_layer(index, incoming, biases, 0, "first", blocks, layers, given=first_tiles)
        own_rows = lax.all_to_all(finished, "section", 0, 0, tiled=True)
    with jax.named_scope("layers"):
        outgoing = pack_rows(index, own_rows, 1, 1, shards, rows, blocks)
        given = None
        for layer in range(1, layers - 1):
            incoming = lax.all_to_all(outgoing, "neuron", 0, 0, tiled=True)
            outgoing, given = run_layer(index, incoming, biases, layer, "inner", blocks, layers, weights, given)
        incoming = lax.all_to_all(outgoing, "neuron", 0, 0, tiled=True)
        return run_layer(index, incoming, biases, layers - 1, "last", blocks, layers, given=given)


def solution(mesh):
    in_specs = (
        P("section", "neuron"),
        P("section", "neuron", None),
        P("section", None),
        P("section", "neuron"),
        P("section", None),
        P("section", "neuron"),
    )
    out_specs = P("section", "neuron")
    return jax.shard_map(body, mesh=mesh, in_specs=in_specs, out_specs=out_specs, check_vma=False)
```

```python
import functools

import jax
import jax.numpy as jnp
from jax import lax
from jax.experimental import pallas as pl
from jax.experimental.pallas import tpu as pltpu
from jax.sharding import PartitionSpec as P

BS = 64
CLAMP_TOP = 32.0
LANES = 128
GROUP = 8
INDEX_STRIDE = 1024
PICKS_AT = 512
VMEM_LIMIT = 44 << 20


def reorder_kernel(in_hbm, out_hbm, in_ref, out_ref, in_sems, out_sems):
    groups, depth, _ = in_ref.shape
    half = depth // GROUP
    pairs = GROUP // 2
    steps = in_sems.shape[0]
    per_step = groups // steps
    spans = [pl.ds(step * per_step, per_step) for step in range(steps)]
    arrivals = [pltpu.make_async_copy(in_hbm.at[span], in_ref.at[span], in_sems.at[step]) for step, span in enumerate(spans)]
    leaves = [pltpu.make_async_copy(out_ref.at[span], out_hbm.at[span], out_sems.at[step]) for step, span in enumerate(spans)]
    for copy in arrivals:
        copy.start()
    row = lax.broadcasted_iota(jnp.int32, (depth, depth), 0)
    col = lax.broadcasted_iota(jnp.int32, (depth, depth), 1)
    parity = row // (pairs * half)
    pair = row // half % pairs
    slab = row % half
    move = (col == slab * GROUP + 2 * pair + parity).astype(jnp.float32).astype(jnp.bfloat16)
    low = lax.broadcasted_iota(jnp.int32, (half, LANES), 1) < BS
    for step in range(steps):
        arrivals[step].wait()
        for group in range(step * per_step, (step + 1) * per_step):
            moved = jnp.dot(move, in_ref[group], preferred_element_type=jnp.float32)
            for pair in range(pairs):
                first = moved[pair * half : (pair + 1) * half]
                second = moved[(pairs + pair) * half : (pairs + pair + 1) * half]
                even = jnp.where(low, first, pltpu.roll(second, BS, 1))
                odd = jnp.where(low, pltpu.roll(first, BS, 1), second)
                at = pair * 2 * half
                out_ref[group, at : at + half, :] = even.astype(out_ref.dtype)
                out_ref[group, at + half : at + 2 * half, :] = odd.astype(out_ref.dtype)
        leaves[step].start()
    for copy in leaves:
        copy.wait()


def reorder_tiles(bands):
    steps = 4
    anywhere = pl.BlockSpec(memory_space=pl.ANY)
    return pl.pallas_call(
        reorder_kernel,
        in_specs=[anywhere],
        out_specs=anywhere,
        out_shape=jax.ShapeDtypeStruct(bands.shape, bands.dtype),
        scratch_shapes=[
            pltpu.VMEM(bands.shape, bands.dtype),
            pltpu.VMEM(bands.shape, bands.dtype),
            pltpu.SemaphoreType.DMA((steps,)),
            pltpu.SemaphoreType.DMA((steps,)),
        ],
        compiler_params=pltpu.CompilerParams(vmem_limit_bytes=62 << 20),
        name="reorder_tiles",
    )(bands)


def parity_position(lane):
    within = lane % BS
    return 2 * (within % (BS // 2)) + within // (BS // 2)


def spread_matrix(offset):
    row = lax.broadcasted_iota(jnp.int32, (LANES, 2 * LANES), 0)
    col = lax.broadcasted_iota(jnp.int32, (LANES, 2 * LANES), 1)
    lane = col % LANES
    wanted_half = (col // LANES) == (lane // BS)
    hit = wanted_half & (row == parity_position(lane) + offset)
    return hit.astype(jnp.float32).astype(jnp.bfloat16)


def pack_blocks(index_ref, picks_at, low_ref, high_ref, out_ref):
    for shard in range(out_ref.shape[0]):
        first = index_ref[picks_at + 2 * shard]
        second = index_ref[picks_at + LANES + 2 * shard]
        out_ref[shard] = low_ref[first] + high_ref[second]


def pack_kernel(at, sources, index_hbm, *refs):
    *in_refs, out_ref, index_ref, low_ref, high_ref, index_sem = refs
    chunk = out_ref.shape[1] // sources
    index_copy = pltpu.make_async_copy(index_hbm.at[pl.ds(at * INDEX_STRIDE, INDEX_STRIDE)], index_ref, index_sem)
    index_copy.start()
    section = lax.axis_index("section")
    matrices = [spread_matrix(offset * BS) for offset in range(2)]
    for tile in range(low_ref.shape[0] // 2):
        span = pl.ds(tile * chunk, chunk)
        if sources == 1:
            value = in_refs[0][span]
            for chip in range(1, len(in_refs)):
                value = jnp.where(section // 2 == chip, in_refs[chip][span], value)
        else:
            value = jnp.concatenate([in_refs[0][2 * source + section % 2, span] for source in range(sources)], axis=0)
        for offset in range(2):
            spread = jnp.dot(value, matrices[offset], preferred_element_type=jnp.float32).astype(jnp.bfloat16)
            low_ref[2 * tile + offset] = spread[:, :LANES]
            high_ref[2 * tile + offset] = spread[:, LANES:]
    index_copy.wait()
    pack_blocks(index_ref, PICKS_AT, low_ref, high_ref, out_ref)


def pack_rows(index, arrays, at, sources, shards, rows, blocks):
    in_vmem = pl.BlockSpec(memory_space=pltpu.VMEM)
    return pl.pallas_call(
        functools.partial(pack_kernel, at, sources),
        in_specs=[pl.BlockSpec(memory_space=pl.ANY)] + [in_vmem] * len(arrays),
        out_specs=in_vmem,
        scratch_shapes=[
            pltpu.SMEM((INDEX_STRIDE,), jnp.int32),
            pltpu.VMEM((blocks, rows, LANES), jnp.bfloat16),
            pltpu.VMEM((blocks, rows, LANES), jnp.bfloat16),
            pltpu.SemaphoreType.DMA,
        ],
        out_shape=jax.ShapeDtypeStruct((shards, rows, LANES), jnp.bfloat16),
        compiler_params=pltpu.CompilerParams(vmem_limit_bytes=VMEM_LIMIT),
        name="pack_rows",
    )(index, *arrays)


def layer_kernel(layer, kind, fetch, ahead, *refs):
    refs = list(refs)
    index_hbm, in_ref, bias_ref = (refs.pop(0) for _ in range(3))
    given_ref = None if fetch else refs.pop(0)
    weights_hbm = refs.pop(0) if fetch or ahead else None
    out_refs = [refs.pop(0) for _ in range(lax.axis_size("section") // 2 if kind == "first" else 1)]
    out_ref = out_refs[0]
    next_ref = refs.pop(0) if ahead else None
    index_ref, fetched_ref, spread_ref, low_ref, high_ref, index_sem, tile_sems, next_sem, *total_refs = refs
    tiles_ref = fetched_ref if fetch else given_ref
    shards, rows, _ = in_ref.shape
    groups = tiles_ref.shape[0]
    tile_slots = groups * GROUP
    blocks = total_refs[0].shape[0] - 1
    steps = tile_sems.shape[0]
    per_step = groups // steps
    index_copy = pltpu.make_async_copy(
        index_hbm.at[pl.ds(layer * INDEX_STRIDE, index_ref.shape[0])], index_ref, index_sem
    )
    index_copy.start()

    def tile_copy(source, step):
        span = pl.ds(step * per_step, per_step)
        return pltpu.make_async_copy(source.at[span], fetched_ref.at[span], tile_sems.at[step])

    if fetch:
        tiles_hbm = weights_hbm.at[layer]
        for step in range(steps):
            tile_copy(tiles_hbm, step).start()
    if ahead:
        next_copy = pltpu.make_async_copy(weights_hbm.at[layer + 1], next_ref, next_sem)
        next_copy.start()
    for total_ref in total_refs:
        total_ref[...] = jnp.zeros_like(total_ref)
    low = lax.broadcasted_iota(jnp.int32, (rows, LANES), 1) < BS
    for shard in range(shards):
        value = in_ref[shard].astype(jnp.float32)
        turned = pltpu.roll(value, BS, 1)
        spread_ref[0, 2 * shard] = jnp.where(low, value, 0.0).astype(jnp.bfloat16)
        spread_ref[0, 2 * shard + 1] = jnp.where(low, turned, 0.0).astype(jnp.bfloat16)
        spread_ref[1, 2 * shard] = jnp.where(low, 0.0, turned).astype(jnp.bfloat16)
        spread_ref[1, 2 * shard + 1] = jnp.where(low, 0.0, value).astype(jnp.bfloat16)
    index_copy.wait()
    empty = jnp.zeros((rows, LANES), jnp.bfloat16)
    for group in range(groups):
        if fetch and group % per_step == 0:
            tile_copy(tiles_hbm, group // per_step).wait()
        first_tile = group * GROUP
        left = []
        right = []
        for member in range(GROUP):
            pair = member // 2
            value = spread_ref[pair % 2, index_ref[first_tile + member]]
            left.append(value if pair < 2 else empty)
            right.append(value if pair >= 2 else empty)
        gathered = jnp.concatenate([jnp.concatenate(left, axis=0), jnp.concatenate(right, axis=0)], axis=1)
        product = jnp.dot(gathered, tiles_ref[group], preferred_element_type=jnp.float32)
        for member in range(GROUP):
            column = index_ref[tile_slots + first_tile + member]
            total_refs[member][column] += product[member * rows : (member + 1) * rows]

    even, odd = (
        sum(total_refs[member][:blocks] for member in range(parity, GROUP, 2)).reshape(blocks * rows, LANES)
        for parity in range(2)
    )
    summed = (even + pltpu.roll(odd, BS, 1)).reshape(blocks, rows, LANES) + bias_ref[layer][:, None, :]
    result = jnp.clip(summed, 0.0, CLAMP_TOP)
    if kind == "inner":
        value = jnp.dot(
            result.astype(jnp.bfloat16).reshape(blocks * rows, LANES),
            spread_matrix(0),
            preferred_element_type=jnp.float32,
        ).astype(jnp.bfloat16)
        low_ref[...] = value[:, :LANES].reshape(blocks, rows, LANES)
        high_ref[...] = value[:, LANES:].reshape(blocks, rows, LANES)
        pack_blocks(index_ref, INDEX_STRIDE + PICKS_AT, low_ref, high_ref, out_ref)
        if ahead:
            next_copy.wait()
        return
    low_rows = lax.broadcasted_iota(jnp.int32, (rows, LANES), 1) < BS
    for tile in range(blocks // 2):
        value = jnp.where(low_rows, result[2 * tile], pltpu.roll(result[2 * tile + 1], BS, 1)).astype(out_ref.dtype)
        if kind == "last":
            out_ref[:, tile * LANES : (tile + 1) * LANES] = value
        else:
            chunk = rows // len(out_refs)
            for chip, chip_ref in enumerate(out_refs):
                chip_ref[tile * chunk : (tile + 1) * chunk] = value[chip * chunk : (chip + 1) * chunk]


def run_layer(index, incoming, bias, layer, kind, blocks, layers, weights=None, given=None):
    shards, rows, _ = incoming.shape
    fetch = given is None
    ahead = kind == "inner"
    groups, depth = (weights if fetch else given).shape[-3:-1]
    steps = 2
    if kind == "first":
        out_shape = (rows // (layers // 2) * blocks // 2, LANES)
    elif kind == "last":
        out_shape = (rows, blocks * BS)
    else:
        out_shape = (shards, rows, LANES)
    in_vmem = pl.BlockSpec(memory_space=pltpu.VMEM)
    anywhere = pl.BlockSpec(memory_space=pl.ANY)
    operands = [(index, anywhere), (incoming, in_vmem), (bias, in_vmem)]
    if not fetch:
        operands.append((given, in_vmem))
    if fetch or ahead:
        operands.append((weights, anywhere))
    results = [jax.ShapeDtypeStruct(out_shape, jnp.bfloat16)] * (layers // 2 if kind == "first" else 1)
    if ahead:
        results.append(jax.ShapeDtypeStruct((groups, depth, LANES), jnp.bfloat16))
    done = pl.pallas_call(
        functools.partial(layer_kernel, layer, kind, fetch, ahead),
        in_specs=[spec for _, spec in operands],
        out_specs=[in_vmem] * len(results),
        scratch_shapes=[
            pltpu.SMEM((2 * INDEX_STRIDE if kind == "inner" else INDEX_STRIDE,), jnp.int32),
            pltpu.VMEM((groups if fetch else 1, depth, LANES), jnp.bfloat16),
            pltpu.VMEM((2, 2 * shards, rows, LANES), jnp.bfloat16),
            pltpu.VMEM((blocks, rows, LANES), jnp.bfloat16),
            pltpu.VMEM((blocks, rows, LANES), jnp.bfloat16),
            pltpu.SemaphoreType.DMA,
            pltpu.SemaphoreType.DMA((steps,)),
            pltpu.SemaphoreType.DMA,
        ]
        + [pltpu.VMEM((blocks + 1, rows, LANES), jnp.float32)] * GROUP,
        out_shape=results,
        compiler_params=pltpu.CompilerParams(vmem_limit_bytes=VMEM_LIMIT),
        cost_estimate=pl.CostEstimate(flops=2 * groups * GROUP * 2 * rows * depth * LANES, bytes_accessed=3 << 20, transcendentals=0),
        name="layer_step",
    )(*[operand for operand, _ in operands])
    return done if len(results) > 1 else done[0]


def plan_kernel(blocks_dev, count_ref, rows_ref, cols_ref, counts_ref, bias_ref, in_ref, out_ref):
    own = lax.axis_index("neuron")
    per_shard = cols_ref.shape[0]
    lane = lax.broadcasted_iota(jnp.int32, (LANES, LANES), 1)
    sub = lax.broadcasted_iota(jnp.int32, (LANES, LANES), 0)
    unused = 1 << 16
    own_rows = rows_ref[pl.ds(own * per_shard, per_shard), :]
    slot_ids = lax.broadcasted_iota(jnp.int32, (per_shard, LANES), 0) * LANES + lax.broadcasted_iota(
        jnp.int32, (per_shard, LANES), 1
    )
    used = slot_ids < count_ref[own]
    known = jnp.where(used, own_rows, unused)
    across = [jnp.broadcast_to(own_rows[half : half + 1], (LANES, LANES)) for half in range(per_shard)]
    down = [
        jnp.broadcast_to(known[half : half + 1].astype(jnp.float32), (LANES, LANES)).T.astype(jnp.int32)
        for half in range(per_shard)
    ]
    ranks = []
    for here in across:
        earlier = jnp.zeros((1, LANES), jnp.int32)
        for there in down:
            hit = (there // blocks_dev == here // blocks_dev) & (there < here)
            earlier = jnp.maximum(earlier, jnp.max(hit.astype(jnp.int32), axis=0, keepdims=True))
        ranks.append(earlier)
    rank = jnp.concatenate(ranks, axis=0)
    slot = jnp.where(used, 2 * (own_rows // blocks_dev) + rank, 0)
    column = jnp.where(used, cols_ref[...], blocks_dev)
    shards = counts_ref.shape[1]
    shard_lane = lax.broadcasted_iota(jnp.int32, (LANES, shards), 1)
    shard_sub = lax.broadcasted_iota(jnp.int32, (LANES, shards), 0) // per_shard
    counts = jnp.sum(
        jnp.where(shard_lane == shard_sub, jnp.broadcast_to(counts_ref[...], (LANES, shards)), 0).astype(jnp.float32),
        axis=1,
        keepdims=True,
    ).astype(jnp.int32)
    rows = rows_ref[...]
    wanted = (rows // blocks_dev == own) & ((sub % per_shard) * LANES + lane < counts)
    local = rows - own * blocks_dev
    lowest = jnp.min(jnp.where(wanted, local, blocks_dev - 1).astype(jnp.float32), axis=1, keepdims=True)
    highest = jnp.max(jnp.where(wanted, local, 0).astype(jnp.float32), axis=1, keepdims=True)
    lowest = jnp.broadcast_to(lowest, (LANES, LANES)).T[:8]
    highest = jnp.broadcast_to(highest, (LANES, LANES)).T[:8]
    lowest = jnp.minimum(lowest, pltpu.roll(lowest, LANES - 1, 1))
    highest = jnp.maximum(highest, pltpu.roll(highest, LANES - 1, 1))
    numbers = [slot.astype(jnp.float32), column.astype(jnp.float32), lowest[:1], highest[:1]]
    numbers.append(jnp.zeros((14 - 2 * per_shard, LANES), jnp.float32))
    bias = bias_ref[...]
    rounded = bias.astype(jnp.bfloat16)
    rest = bias - rounded.astype(jnp.float32)
    rest_rounded = rest.astype(jnp.bfloat16)
    last = (rest - rest_rounded.astype(jnp.float32)).astype(jnp.bfloat16)
    small = jnp.concatenate(numbers, axis=0).astype(jnp.bfloat16)
    parts = jnp.concatenate([rounded.astype(jnp.float32), rest_rounded.astype(jnp.float32)], axis=0).astype(jnp.bfloat16)
    ends = jnp.concatenate([last.astype(jnp.float32), jnp.zeros_like(bias)], axis=0).astype(jnp.bfloat16)
    rows_in, width = in_ref.shape
    for target in range(out_ref.shape[0]):
        for tile in range(width // LANES):
            out_ref[target, tile * rows_in : (tile + 1) * rows_in] = in_ref[:, tile * LANES : (tile + 1) * LANES]
        at = rows_in * width // LANES
        for piece in (small, parts, ends):
            out_ref[target, at : at + piece.shape[0]] = piece
            at += piece.shape[0]


def plan_routes(tile_row, tile_col, tile_count, bias, features, blocks_dev, layers):
    rows, width = features.shape
    in_vmem = pl.BlockSpec(memory_space=pltpu.VMEM)
    return pl.pallas_call(
        functools.partial(plan_kernel, blocks_dev),
        in_specs=[pl.BlockSpec(memory_space=pltpu.SMEM)] + [in_vmem] * 5,
        out_specs=in_vmem,
        out_shape=jax.ShapeDtypeStruct((layers, rows * width // LANES + 48, LANES), jnp.bfloat16),
        cost_estimate=pl.CostEstimate(flops=0, bytes_accessed=4 << 20, transcendentals=0),
        name="plan_routes",
    )(
        tile_count[0],
        tile_row.reshape(-1, LANES),
        tile_col.reshape(-1, LANES),
        tile_count,
        bias.reshape(-1, LANES),
        features,
    )


def body(features, tiles, tile_row, tile_col, tile_count, bias):
    shards = lax.axis_size("neuron")
    layers = lax.axis_size("section")
    rows, width = features.shape
    blocks = width // BS
    tile_slots = tiles.shape[1]
    to_odd = [(source, source + 1) for source in range(0, layers, 2)]
    with jax.named_scope("tile_order"):
        slabs = tiles[0].reshape(tile_slots // GROUP, GROUP, BS * BS // LANES, LANES)
        bands = slabs.transpose(0, 2, 1, 3).reshape(tile_slots // GROUP, GROUP * BS // 2, LANES)
        ordered = reorder_tiles(bands)
    with jax.named_scope("weight_gather"):
        weights = lax.all_gather(ordered, "section", axis=0)
    with jax.named_scope("routes"):
        plan = plan_routes(tile_row, tile_col, tile_count, bias, features, blocks, layers)
        shared = lax.all_to_all(plan, "section", 0, 0, tiled=True)
        at = rows * width // LANES
        index = shared[:, at : at + 8].astype(jnp.int32).reshape(-1)
        parts = [shared[:, at + start : at + start + 8].astype(jnp.float32) for start in (16, 24, 32)]
        biases = (parts[0] + parts[1] + parts[2]).reshape(layers, blocks, BS)
        biases = jnp.pad(biases, ((0, 0), (0, 0), (0, LANES - BS)))
    with jax.named_scope("first_layer"):
        sent = lax.ppermute(ordered, "section", to_odd)
        first_tiles = jnp.where(lax.axis_index("section") % 2 == 0, ordered, sent)
        outgoing = pack_rows(index, [shared], 0, layers // 2, shards, rows * layers // 2, blocks)
        incoming = lax.all_to_all(outgoing, "neuron", 0, 0, tiled=True)
        finished = run_layer(index, incoming, biases, 0, "first", blocks, layers, given=first_tiles)
        own_rows = [finished[0]] + [
            lax.ppermute(finished[chip], "section", [(core, 2 * chip + core) for core in range(2)])
            for chip in range(1, layers // 2)
        ]
    with jax.named_scope("layers"):
        outgoing = pack_rows(index, own_rows, 1, 1, shards, rows, blocks)
        given = None
        for layer in range(1, layers - 1):
            incoming = lax.all_to_all(outgoing, "neuron", 0, 0, tiled=True)
            outgoing, given = run_layer(index, incoming, biases, layer, "inner", blocks, layers, weights, given)
        incoming = lax.all_to_all(outgoing, "neuron", 0, 0, tiled=True)
        return run_layer(index, incoming, biases, layers - 1, "last", blocks, layers, given=given)


def solution(mesh):
    in_specs = (
        P("section", "neuron"),
        P("section", "neuron", None),
        P("section", None),
        P("section", "neuron"),
        P("section", None),
        P("section", "neuron"),
    )
    out_specs = P("section", "neuron")
    return jax.shard_map(body, mesh=mesh, in_specs=in_specs, out_specs=out_specs, check_vma=False)
```
